256 devices in a mesh: dp: 64 (over z, y, core), tensor: 4 (over x).
Axes of the slice: x: 4, y: 4, z: 8, core: 2. Of those that a mesh axis runs over, the one named last changes fastest.
Arguments:
- gradient: bfloat16 [8, 32, 1024, 1024], P(None, 'tensor', 'dp'), may hold values from -6 to 6
- owner: int32 [256], replicated, may hold values from 0 to 255, as said below
- left_root: bfloat16 [256, 1024, 1024], P(('dp', 'tensor')), as said below
- right_root: bfloat16 [256, 1024, 1024], P(('dp', 'tensor')), as said below
Outputs:
- left_gram: bfloat16 [256, 1024, 1024], P(('dp', 'tensor'))
- right_gram: bfloat16 [256, 1024, 1024], P(('dp', 'tensor'))
- update: bfloat16 [8, 32, 1024, 1024], P(None, 'tensor', 'dp')
The draws below stay inside these ranges and needn't reach their ends.
Inputs may be any that keep to these rules, and one draw needn't show every extreme that they name: owner is a permutation of the devices; the 64 blocks of one tensor slab have 64 different owner dp indices, and each tensor index owns 64 // 4 of them. `left_root`: symmetric, positive definite. `right_root`: symmetric, positive definite.
All inputs are finite; a program needn't handle non-finite values.
Results may differ from the reference program's by a relative error of at most 0.0049.
Values may be sent and summed in bfloat16 or wider, within the bound.
A program may use at most 128 MiB of HBM per device.

```python
import jax
import jax.numpy as jnp
from jax import lax

BS = 1024
BR = 8
BC = 32
BLOCKS = 256
N_DP = 64
N_TENSOR = 4


def root_matrix(key, diag_low, diag_high, spread):
    diag_key, off_key = jax.random.split(key)
    diagonal = jax.random.uniform(diag_key, (BLOCKS, BS), jnp.float32, diag_low, diag_high)
    rough = jax.random.normal(off_key, (BLOCKS, BS, BS), jnp.float32) * (spread / BS ** 0.5)
    symmetric = (rough + jnp.swapaxes(rough, 1, 2)) * 0.5 ** 0.5
    eye = jnp.eye(BS, dtype=jnp.float32)
    return symmetric + diagonal[:, :, None] * eye[None, :, :]


def draw_left_root(key, part):
    key = jax.random.fold_in(key, 11)
    return root_matrix(key, 1.0, 2.5, 0.35).astype(jnp.bfloat16)


def draw_right_root(key, part):
    key = jax.random.fold_in(key, 23)
    return root_matrix(key, 1.0, 2.5, 0.35).astype(jnp.bfloat16)


def draw_owner(key, part):
    key = jax.random.fold_in(key, 37)
    perm_key, class_key = jax.random.split(key)
    slab_keys = jax.random.split(perm_key, N_TENSOR)
    owner_dp = jax.vmap(lambda single: jax.random.permutation(single, N_DP))(slab_keys)
    classes = jax.random.permutation(class_key, N_DP) % N_TENSOR
    slab_index = jnp.arange(N_TENSOR, dtype=jnp.int32)[:, None]
    owner_ten = (slab_index + classes[owner_dp]) % N_TENSOR
    return (owner_dp * N_TENSOR + owner_ten).reshape(BLOCKS).astype(jnp.int32)


def shard_levels(rng, dims, shards, least, top_value):
    def one(position, blocks):
        heights = jax.random.uniform(jax.random.fold_in(jax.random.fold_in(rng, 6), position), (blocks,), jnp.float32, least / len(shards), top_value / len(shards))
        return jnp.repeat(jnp.exp(heights), dims[position] // blocks).reshape((-1,) + (1,) * (len(dims) - position - 1))

    level = one(*shards[0])
    for cut in shards[1:]:
        level = level * one(*cut)
    return level


def gaussian(stream_key, extent, scale, bound, shards=(), held_as=jnp.bfloat16):
    loudness = shard_levels(stream_key, extent, shards, -0.22, 0.18) if shards else 1.0
    entries = jax.random.normal(stream_key, extent, jnp.float32) * scale * loudness
    return jnp.minimum(jnp.maximum(entries, -bound), bound).astype(held_as)


def setup_inputs(seed: int = 0) -> dict:
    streams_of = jax.random.split(jax.random.key(seed), 5)
    return {
        "gradient": gaussian(streams_of[0], (BR, BC, BS, BS), 1.0, 6.0, ((1, 4), (2, 64))),
        "owner": draw_owner(jax.random.fold_in(streams_of[4], 71), 0),
        "left_root": draw_left_root(jax.random.fold_in(streams_of[4], 71), 0),
        "right_root": draw_right_root(jax.random.fold_in(streams_of[4], 71), 0),
    }


def owner_work(tile_data, left_piece, right_piece):
    left_new = (jnp.dot(tile_data, tile_data.T, preferred_element_type=jnp.float32) / BS).astype(jnp.bfloat16)
    right_new = (jnp.dot(tile_data.T, tile_data, preferred_element_type=jnp.float32) / BS).astype(jnp.bfloat16)
    mixed = jnp.dot(tile_data, right_piece, preferred_element_type=jnp.float32).astype(jnp.bfloat16)
    product = jnp.dot(left_piece, mixed, preferred_element_type=jnp.float32)
    grad_sq = jnp.mean(jnp.square(tile_data.astype(jnp.float32)))
    prod_sq = jnp.mean(jnp.square(product))
    scale = jnp.sqrt(grad_sq) / jnp.sqrt(prod_sq + 1e-06)
    return (left_new, right_new, (product * scale).astype(jnp.bfloat16))

def reference(gradient, owner, left_root, right_root):
    per_slab = BC // N_TENSOR
    tiles = gradient.reshape(BR, N_TENSOR, per_slab, BS, BS).transpose(1, 0, 2, 3, 4).reshape(BLOCKS, BS, BS)

    def one_block(index):
        target = owner[index]
        return owner_work(tiles[index], left_root[target], right_root[target])
    left_new, right_new, updates = lax.map(one_block, jnp.arange(BLOCKS, dtype=jnp.int32))
    left_gram = jnp.zeros((BLOCKS, BS, BS), jnp.bfloat16).at[owner].set(left_new)
    right_gram = jnp.zeros((BLOCKS, BS, BS), jnp.bfloat16).at[owner].set(right_new)
    update = updates.reshape(N_TENSOR, BR, per_slab, BS, BS).transpose(1, 0, 2, 3, 4).reshape(BR, BC, BS, BS)
    return (left_gram, right_gram, update)
```

```python
import functools

import jax
import jax.numpy as jnp
from jax import lax
from jax.experimental import pallas as pl
from jax.experimental.pallas import tpu as pltpu
from jax.sharding import PartitionSpec as P

MESH = pl.DeviceIdType.MESH
CHUNKS = 4
ROW_TILE = 256


def plan(owner, my_ten, n_dp, n_ten):
    group = n_dp // n_ten
    ten = (owner % n_ten).reshape(n_ten, n_dp)
    dp = (owner // n_ten).reshape(n_ten, n_dp)
    place = jnp.arange(n_dp, dtype=jnp.int32)
    earlier = place[None, :] < place[:, None]
    same = ten[:, :, None] == ten[:, None, :]
    rank = jnp.sum((same & earlier[None]).astype(jnp.int32), axis=2)
    home_slot = lax.dynamic_index_in_dim(ten * group + rank, my_ten, 0, keepdims=False)
    out_order = jnp.sum(jnp.where(home_slot[None, :] == place[:, None], place[None, :], 0), axis=1)
    slab = jnp.arange(n_ten, dtype=jnp.int32)[:, None]
    here = jnp.where(ten == my_ten, slab * group + rank, -1).reshape(1, -1)
    here_dp = jnp.where(ten == my_ten, dp, -1).reshape(1, -1)
    by_dp = jnp.sum(jnp.where(here_dp == place[:, None], here, 0), axis=1)
    by_slot = jnp.sum(jnp.where(here == place[:, None], here_dp, 0), axis=1)
    return jnp.stack([out_order, by_dp, by_slot, home_slot]).astype(jnp.int32)


def step_kernel(
    n_dp, n_ten, idx, grad, left_root, right_root,
    left_out, right_out, update_out,
    *scratch,
):
    nc = CHUNKS
    (g_in, p1, a1, p2, tile, left_v, right_v, mixed, prod, upd, h3, q4, r4, out_v, gram_l, gram_r,
     load_sem, x1_send, x1_recv, z_send, z_recv, b_send, b_recv, x4_send, x4_recv, out_sem) = (
        scratch[0:nc], scratch[nc:2 * nc], scratch[2 * nc:3 * nc], scratch[3 * nc:4 * nc],
        *scratch[4 * nc:4 * nc + 6],
        scratch[4 * nc + 6:5 * nc + 6], scratch[5 * nc + 6:6 * nc + 6], scratch[6 * nc + 6:7 * nc + 6],
        *scratch[7 * nc + 6:],
    )
    group = n_dp // n_ten
    rows, width = grad.shape[1], grad.shape[2]
    cw = width // nc
    me = lax.axis_index("dp")
    my_ten = lax.axis_index("tensor")
    core = lax.rem(me, 2)
    chip = me // 2
    n_chip = n_dp // 2

    def cols(c):
        return slice(c * cw, (c + 1) * cw)

    loads = [
        pltpu.make_async_copy(grad.at[:, :, cols(c)], g_in[c], load_sem.at[c]) for c in range(nc)
    ]
    load_right = pltpu.make_async_copy(right_root, right_v, load_sem.at[nc])
    load_left = pltpu.make_async_copy(left_root, left_v, load_sem.at[nc + 1])
    for copy in loads:
        copy.start()
    load_right.start()
    load_left.start()

    barrier = pltpu.get_barrier_semaphore()

    def greet_dp(k, carry):
        pl.semaphore_signal(
            barrier, inc=1, device_id=(lax.rem(me + k, n_dp), my_ten), device_id_type=MESH
        )
        return carry

    def greet_ten(k, carry):
        pl.semaphore_signal(
            barrier, inc=1, device_id=(me, lax.rem(my_ten + k, n_ten)), device_id_type=MESH
        )
        return carry

    lax.fori_loop(1, n_ten, greet_ten, 0)
    lax.fori_loop(1, n_dp, greet_dp, 0)

    def move(dst, dst_base, src, which, idx_base, count):
        def body(j, carry):
            dst[dst_base + j] = src[idx[which, idx_base + j]]
            return carry

        lax.fori_loop(0, count, body, 0, unroll=8)

    def pack_ten(c):
        loads[c].wait()
        for k in (2, 1, 3):
            to = lax.rem(my_ten + k, n_ten)
            move(p1[c], to * group, g_in[c], 0, to * group, group)
        move(a1[c], my_ten * group, g_in[c], 0, my_ten * group, group)

    def ten_copy(c, k, src, dst, send, recv):
        to = lax.rem(my_ten + k, n_ten)
        return pltpu.make_async_remote_copy(
            src_ref=src[c].at[pl.ds(to * group, group)],
            dst_ref=dst[c].at[pl.ds(my_ten * group, group)],
            send_sem=send.at[c],
            recv_sem=recv.at[c],
            device_id=(me, to),
            device_id_type=MESH,
        )

    def send_ten(c, src, dst, send, recv):
        for k in (2, 1, 3):
            ten_copy(c, k, src, dst, send, recv).start()

    def wait_bytes(ref, sem):
        pltpu.make_async_copy(ref, ref, sem).wait()

    others = (n_ten - 1) * group

    pack_ten(0)
    pl.semaphore_wait(barrier, n_dp + n_ten - 2)
    send_ten(0, p1, a1, x1_send, x1_recv)
    for c in range(1, nc):
        pack_ten(c)
        send_ten(c, p1, a1, x1_send, x1_recv)

    def strip_rows(d):
        return pl.ds(pl.multiple_of(d * rows, rows), rows)

    def forward(c, to):
        return pltpu.make_async_remote_copy(
            src_ref=p2[c].at[to],
            dst_ref=tile.at[strip_rows(me), cols(c)],
            send_sem=z_send.at[c],
            recv_sem=z_recv.at[c],
            device_id=(to, my_ten),
            device_id_type=MESH,
        )

    def forward_class(c, k):
        def body(i, carry):
            forward(c, lax.rem(chip + i, n_chip) * 2 + k).start()
            return carry

        lax.fori_loop(1, n_chip, body, 0)

        @pl.when(core != k)
        def _():
            forward(c, chip * 2 + k).start()

        @pl.when(core == k)
        def _():
            pltpu.make_async_copy(
                p2[c].at[me], tile.at[strip_rows(me), cols(c)], z_recv.at[c]
            ).start()

    for c in range(nc):
        wait_bytes(a1[c].at[pl.ds(0, others)], x1_recv.at[c])
        move(p2[c], 0, a1[c], 1, 0, n_dp)
        forward_class(c, 0)
    for c in range(nc):
        forward_class(c, 1)

    load_right.wait()
    load_left.wait()
    for c in range(nc):
        wait_bytes(tile.at[:, cols(c)], z_recv.at[c])

    tiles = width // ROW_TILE

    def row_tile(r):
        return pl.ds(pl.multiple_of(r * ROW_TILE, ROW_TILE), ROW_TILE)

    def mix(r, total):
        g = tile[row_tile(r), :]
        mixed[row_tile(r), :] = jnp.dot(
            g, right_v[...], preferred_element_type=jnp.float32
        ).astype(jnp.bfloat16)
        g = g.astype(jnp.float32)
        return total + jnp.sum(g * g, axis=0, keepdims=True)

    def precondition(r, total):
        p = jnp.dot(left_v[row_tile(r), :], mixed[...], preferred_element_type=jnp.float32)
        prod[row_tile(r), :] = p
        return total + jnp.sum(p * p, axis=0, keepdims=True)

    zero = jnp.zeros((1, width), jnp.float32)
    grad_sum = lax.fori_loop(0, tiles, mix, zero)
    prod_sum = lax.fori_loop(0, tiles, precondition, zero)
    entries = width * width
    grad_sq = jnp.sum(grad_sum, axis=1, keepdims=True) / entries
    prod_sq = jnp.sum(prod_sum, axis=1, keepdims=True) / entries
    scale = jnp.sqrt(grad_sq) / jnp.sqrt(prod_sq + 1e-06)

    def graft(r, carry):
        upd[row_tile(r), :] = (prod[row_tile(r), :] * scale).astype(jnp.bfloat16)
        return carry

    lax.fori_loop(0, tiles, graft, 0)

    def back(c, to):
        return pltpu.make_async_remote_copy(
            src_ref=upd.at[strip_rows(to), cols(c)],
            dst_ref=h3[c].at[me],
            send_sem=b_send.at[c],
            recv_sem=b_recv.at[c],
            device_id=(to, my_ten),
            device_id_type=MESH,
        )

    for c in range(nc):

        def send_back(i, carry, c=c):
            back(c, lax.rem(me + i, n_dp)).start()
            return carry

        lax.fori_loop(1, n_dp, send_back, 0)
        pltpu.make_async_copy(
            upd.at[strip_rows(me), cols(c)], h3[c].at[me], b_recv.at[c]
        ).start()

    def left_stat(r, carry):
        new = lax.dot_general(
            tile[row_tile(r), :], tile[...], (((1,), (1,)), ((), ())),
            preferred_element_type=jnp.float32,
        )
        gram_l[row_tile(r), :] = (new / width).astype(jnp.bfloat16)
        return carry

    lax.fori_loop(0, tiles, left_stat, 0)
    copy_left = pltpu.make_async_copy(gram_l, left_out, out_sem.at[0])
    copy_left.start()
    for r in range(tiles):
        part = slice(r * ROW_TILE, (r + 1) * ROW_TILE)
        new = lax.dot_general(
            tile[:, part], tile[...], (((0,), (0,)), ((), ())),
            preferred_element_type=jnp.float32,
        )
        gram_r[part, :] = (new / width).astype(jnp.bfloat16)
    copy_right = pltpu.make_async_copy(gram_r, right_out, out_sem.at[1])
    copy_right.start()

    def finish(c):
        wait_bytes(r4[c].at[pl.ds(0, others)], x4_recv.at[c])
        move(out_v.at[c], 0, r4[c], 3, 0, n_dp)
        copy = pltpu.make_async_copy(out_v.at[c], update_out.at[:, :, cols(c)], out_sem.at[2 + c])
        copy.start()
        return copy

    results = []
    for c in range(nc):
        wait_bytes(h3[c], b_recv.at[c])
        for k in (2, 1, 3):
            to = lax.rem(my_ten + k, n_ten)
            move(q4[c], to * group, h3[c], 2, to * group, group)
            ten_copy(c, k, q4, r4, x4_send, x4_recv).start()
        move(r4[c], my_ten * group, h3[c], 2, my_ten * group, group)
        if c > 0:
            results.append(finish(c - 1))
    results.append(finish(nc - 1))

    for c in range(nc):
        wait_bytes(p1[c].at[pl.ds(0, others)], x1_send.at[c])
        wait_bytes(p2[c].at[pl.ds(0, n_dp - 1)], z_send.at[c])
        wait_bytes(h3[c].at[pl.ds(0, n_dp - 1)], b_send.at[c])
        wait_bytes(q4[c].at[pl.ds(0, others)], x4_send.at[c])
    copy_left.wait()
    copy_right.wait()
    for copy in results:
        copy.wait()


def shards(gradient, owner, left_root, right_root):
    n_dp = lax.axis_size("dp")
    n_ten = lax.axis_size("tensor")
    my_ten = lax.axis_index("tensor")
    rows, width = gradient.shape[2:]
    cw = width // CHUNKS
    idx = plan(owner, my_ten, n_dp, n_ten)
    chunk = [pltpu.VMEM((n_dp, rows, cw), jnp.bfloat16)] * CHUNKS
    square = pltpu.VMEM((width, width), jnp.bfloat16)
    sems = pltpu.SemaphoreType.DMA((CHUNKS,))
    whole = jax.ShapeDtypeStruct((width, width), jnp.bfloat16)
    left_new, right_new, update = pl.pallas_call(
        functools.partial(step_kernel, n_dp, n_ten),
        out_shape=(whole, whole, jax.ShapeDtypeStruct((n_dp, rows, width), jnp.bfloat16)),
        in_specs=[pl.BlockSpec(memory_space=pltpu.SMEM)] + [pl.BlockSpec(memory_space=pl.ANY)] * 3,
        out_specs=(pl.BlockSpec(memory_space=pl.ANY),) * 3,
        scratch_shapes=[
            *chunk, *chunk, *chunk, *chunk,
            square, square, square, square,
            pltpu.VMEM((width, width), jnp.float32),
            square,
            *chunk, *chunk, *chunk,
            pltpu.VMEM((CHUNKS, n_dp, rows, cw), jnp.bfloat16),
            square, square,
            pltpu.SemaphoreType.DMA((CHUNKS + 2,)),
            sems, sems, sems, sems, sems, sems, sems, sems,
            pltpu.SemaphoreType.DMA((CHUNKS + 2,)),
        ],
        compiler_params=pltpu.CompilerParams(
            collective_id=0, has_side_effects=True, vmem_limit_bytes=56 << 20
        ),
        name="shampoo_step",
    )(idx, gradient.reshape(n_dp, rows, width), left_root[0], right_root[0])
    return left_new[None], right_new[None], update.reshape(gradient.shape)


def solution(mesh):
    return jax.shard_map(
        shards,
        mesh=mesh,
        in_specs=(
            P(None, "tensor", "dp", None),
            P(),
            P(("dp", "tensor"), None, None),
            P(("dp", "tensor"), None, None),
        ),
        out_specs=(
            P(("dp", "tensor"), None, None),
            P(("dp", "tensor"), None, None),
            P(None, "tensor", "dp", None),
        ),
        check_vma=False,
    )
```

```python
import functools

import jax
import jax.numpy as jnp
from jax import lax
from jax.experimental import pallas as pl
from jax.experimental.pallas import tpu as pltpu
from jax.sharding import PartitionSpec as P

MESH = pl.DeviceIdType.MESH
DIRECT = 128
CHUNKS = (128, 256, 256, 256)
STARTS = tuple(DIRECT + sum(CHUNKS[:c]) for c in range(len(CHUNKS)))
ROW_TILE = 256
OUT_ORDER, BY_DP, BY_SLOT, HOME_SLOT, AT_DP, DP_OF, SLAB_OF, TEN_OF = range(8)


def plan(owner, my_ten, n_dp, n_ten):
    group = n_dp // n_ten
    ten = (owner % n_ten).reshape(n_ten, n_dp)
    dp = (owner // n_ten).reshape(n_ten, n_dp)
    place = jnp.arange(n_dp, dtype=jnp.int32)
    earlier = place[None, :] < place[:, None]
    same = ten[:, :, None] == ten[:, None, :]
    rank = jnp.sum((same & earlier[None]).astype(jnp.int32), axis=2)
    mine = lambda table: lax.dynamic_index_in_dim(table, my_ten, 0, keepdims=False)
    home_slot, dp_of, ten_of = mine(ten * group + rank), mine(dp), mine(ten)
    out_order = jnp.sum(jnp.where(home_slot[None, :] == place[:, None], place[None, :], 0), axis=1)
    at_dp = dp_of[None, :] == place[:, None]
    by_owner_dp = jnp.sum(jnp.where(at_dp, place[None, :], 0), axis=1)
    ten_of_dp = jnp.sum(jnp.where(at_dp, ten_of[None, :], 0), axis=1)
    slab = jnp.arange(n_ten, dtype=jnp.int32)[:, None]
    here = jnp.where(ten == my_ten, slab * group + rank, -1).reshape(1, -1)
    here_dp = jnp.where(ten == my_ten, dp, -1).reshape(1, -1)
    by_dp = jnp.sum(jnp.where(here_dp == place[:, None], here, 0), axis=1)
    by_slot = jnp.sum(jnp.where(here == place[:, None], here_dp, 0), axis=1)
    return jnp.stack(
        [out_order, by_dp, by_slot, home_slot, by_owner_dp, dp_of, by_dp // group, ten_of_dp]
    ).astype(jnp.int32)


def step_kernel(n_dp, n_ten, names, idx, grad, left_root, right_root, gram_l, gram_r, out, *scratch):
    s = dict(zip(names, scratch, strict=True))
    nc = len(CHUNKS)
    g_in, p1, a1, p2, h3, q4, r4 = (
        [s[f"{kind}{c}"] for c in range(nc)] for kind in ("g_in", "p1", "a1", "p2", "h3", "q4", "r4")
    )
    tile, left_v, right_v, mixed, prod, upd = (
        s[k] for k in ("tile", "left_v", "right_v", "mixed", "prod", "upd")
    )
    d_in, d_out, d_block, d_all, u_all, u_out, u_home = (
        s[k] for k in ("d_in", "d_out", "d_block", "d_all", "u_all", "u_out", "u_home")
    )
    load_sem = s["load_sem"]
    group = n_dp // n_ten
    rows, width = grad.shape[1], grad.shape[2]
    me = lax.axis_index("dp")
    my_ten = lax.axis_index("tensor")
    core = lax.rem(me, 2)
    chip = me // 2
    n_chip = n_dp // 2
    direct = slice(0, DIRECT)

    def cols(c):
        return slice(STARTS[c], STARTS[c] + CHUNKS[c])

    load_direct = pltpu.make_async_copy(grad.at[:, :, direct], d_in, load_sem.at[nc])
    loads = [
        pltpu.make_async_copy(grad.at[:, :, cols(c)], g_in[c], load_sem.at[c]) for c in range(nc)
    ]
    load_right = pltpu.make_async_copy(right_root, right_v, load_sem.at[nc + 1])
    load_left = pltpu.make_async_copy(left_root, left_v, load_sem.at[nc + 2])
    for copy in (load_direct, *loads, load_right, load_left):
        copy.start()

    barrier = pltpu.get_barrier_semaphore()

    def greet_dp(k, carry):
        pl.semaphore_signal(
            barrier, inc=1, device_id=(lax.rem(me + k, n_dp), my_ten), device_id_type=MESH
        )
        return carry

    def greet_ten(k, carry):
        pl.semaphore_signal(
            barrier, inc=1, device_id=(me, lax.rem(my_ten + k, n_ten)), device_id_type=MESH
        )
        return carry

    lax.fori_loop(1, n_ten, greet_ten, 0)
    lax.fori_loop(1, n_dp, greet_dp, 0)

    def move(dst, dst_base, src, which, idx_base, count):
        def body(j, carry):
            dst[dst_base + j] = src[idx[which, idx_base + j]]
            return carry

        lax.fori_loop(0, count, body, 0, unroll=8)

    def wait_bytes(ref, sem):
        pltpu.make_async_copy(ref, ref, sem).wait()

    def strip_rows(d):
        return pl.ds(pl.multiple_of(d * rows, rows), rows)

    others = (n_ten - 1) * group

    def ten_copy(c, k, src, dst, send, recv):
        to = lax.rem(my_ten + k, n_ten)
        return pltpu.make_async_remote_copy(
            src_ref=src[c].at[pl.ds(to * group, group)],
            dst_ref=dst[c].at[pl.ds(my_ten * group, group)],
            send_sem=s[send].at[c],
            recv_sem=s[recv].at[c],
            device_id=(me, to),
            device_id_type=MESH,
        )

    def send_ten(c, packed, arrived, src, which, send, recv):
        for k in (2, 1, 3):
            to = lax.rem(my_ten + k, n_ten)
            move(packed[c], to * group, src[c], which, to * group, group)
            ten_copy(c, k, packed, arrived, send, recv).start()
        move(arrived[c], my_ten * group, src[c], which, my_ten * group, group)

    def send_whole(src, dst, send, recv):
        for k in (2, 1, 3):
            pltpu.make_async_remote_copy(
                src_ref=src,
                dst_ref=dst.at[my_ten],
                send_sem=s[send].at[0],
                recv_sem=s[recv].at[0],
                device_id=(me, lax.rem(my_ten + k, n_ten)),
                device_id_type=MESH,
            ).start()

    def send_class(copy, local, k):
        def body(i, carry):
            copy(lax.rem(chip + i, n_chip) * 2 + k).start()
            return carry

        lax.fori_loop(1, n_chip, body, 0)

        @pl.when(core != k)
        def _():
            copy(chip * 2 + k).start()

        @pl.when(core == k)
        def _():
            local().start()

    def dp_copy(src, dst, send, recv, to):
        return pltpu.make_async_remote_copy(
            src_ref=src, dst_ref=dst, send_sem=send, recv_sem=recv,
            device_id=(to, my_ten), device_id_type=MESH,
        )

    def forward_direct(to):
        return dp_copy(d_out.at[to], d_block.at[me], s["d_send"].at[0], s["d_recv"].at[0], to)

    def forward_direct_local():
        return pltpu.make_async_copy(d_out.at[me], d_block.at[me], s["d_recv"].at[0])

    def forward(c, to):
        return dp_copy(
            p2[c].at[to], tile.at[strip_rows(me), cols(c)], s["z_send"].at[c], s["z_recv"].at[c], to
        )

    def forward_local(c):
        return pltpu.make_async_copy(
            p2[c].at[me], tile.at[strip_rows(me), cols(c)], s["z_recv"].at[c]
        )

    load_direct.wait()
    move(d_out, 0, d_in, AT_DP, 0, n_dp)
    loads[0].wait()
    pl.semaphore_wait(barrier, n_dp + n_ten - 2)
    for k in range(2):
        send_class(forward_direct, forward_direct_local, k)
    for c in range(nc):
        if c > 0:
            loads[c].wait()
        send_ten(c, p1, a1, g_in, OUT_ORDER, "x1_send", "x1_recv")

    for c in range(nc):
        wait_bytes(a1[c].at[pl.ds(0, others)], s["x1_recv"].at[c])
        move(p2[c], 0, a1[c], BY_DP, 0, n_dp)
        send_class(functools.partial(forward, c), functools.partial(forward_local, c), 0)
    for c in range(nc):
        send_class(functools.partial(forward, c), functools.partial(forward_local, c), 1)

    wait_bytes(d_block, s["d_recv"].at[0])
    send_whole(d_block, d_all, "e_send", "e_recv")

    def keep(i, carry):
        d_all[my_ten, i] = d_block[i]
        return carry

    lax.fori_loop(0, n_dp, keep, 0, unroll=8)
    wait_bytes(d_all.at[pl.ds(0, n_ten - 1)], s["e_recv"].at[0])
    slab = idx[SLAB_OF, me]

    def take(i, carry):
        tile[strip_rows(i), direct] = d_all[slab, i]
        return carry

    lax.fori_loop(0, n_dp, take, 0, unroll=8)

    load_right.wait()
    load_left.wait()
    for c in range(nc):
        wait_bytes(tile.at[:, cols(c)], s["z_recv"].at[c])

    tiles = width // ROW_TILE

    def row_tile(r):
        return pl.ds(pl.multiple_of(r * ROW_TILE, ROW_TILE), ROW_TILE)

    def mix(r, total):
        g = tile[row_tile(r), :]
        mixed[row_tile(r), :] = jnp.dot(
            g, right_v[...], preferred_element_type=jnp.float32
        ).astype(jnp.bfloat16)
        g = g.astype(jnp.float32)
        return total + jnp.sum(g * g, axis=0, keepdims=True)

    def precondition(r, total):
        p = jnp.dot(left_v[row_tile(r), :], mixed[...], preferred_element_type=jnp.float32)
        prod[row_tile(r), :] = p
        return total + jnp.sum(p * p, axis=0, keepdims=True)

    zero = jnp.zeros((1, width), jnp.float32)
    grad_sum = lax.fori_loop(0, tiles, mix, zero)
    prod_sum = lax.fori_loop(0, tiles, precondition, zero)
    entries = width * width
    grad_sq = jnp.sum(grad_sum, axis=1, keepdims=True) / entries
    prod_sq = jnp.sum(prod_sum, axis=1, keepdims=True) / entries
    scale = jnp.sqrt(grad_sq) / jnp.sqrt(prod_sq + 1e-06)

    def graft(r, carry):
        upd[row_tile(r), :] = (prod[row_tile(r), :] * scale).astype(jnp.bfloat16)
        return carry

    lax.fori_loop(0, tiles, graft, 0)

    def keep_update(i, carry):
        u_all[my_ten, i] = upd[strip_rows(i), direct]
        return carry

    lax.fori_loop(0, n_dp, keep_update, 0, unroll=8)
    send_whole(u_all.at[my_ten], u_all, "f_send", "f_recv")

    order = range(nc - 1, -1, -1)
    for c in order:

        def send_back(i, carry, c=c):
            to = lax.rem(me + i, n_dp)
            dp_copy(
                upd.at[strip_rows(to), cols(c)], h3[c].at[me],
                s["b_send"].at[c], s["b_recv"].at[c], to,
            ).start()
            return carry

        lax.fori_loop(1, n_dp, send_back, 0)
        pltpu.make_async_copy(
            upd.at[strip_rows(me), cols(c)], h3[c].at[me], s["b_recv"].at[c]
        ).start()

    def left_stat(r, carry):
        new = lax.dot_general(
            tile[row_tile(r), :], tile[...], (((1,), (1,)), ((), ())),
            preferred_element_type=jnp.float32,
        )
        gram_l[row_tile(r), :] = (new / width).astype(jnp.bfloat16)
        return carry

    lax.fori_loop(0, tiles, left_stat, 0)

    wait_bytes(u_all.at[pl.ds(0, n_ten - 1)], s["f_recv"].at[0])
    ten = idx[TEN_OF, me]

    def take_update(i, carry):
        u_out[i] = u_all[ten, i]
        return carry

    lax.fori_loop(0, n_dp, take_update, 0, unroll=8)

    def send_home(i, carry):
        to = lax.rem(me + i, n_dp)
        dp_copy(u_out.at[to], u_home.at[me], s["h_send"].at[0], s["h_recv"].at[0], to).start()
        return carry

    lax.fori_loop(1, n_dp, send_home, 0)
    pltpu.make_async_copy(u_out.at[me], u_home.at[me], s["h_recv"].at[0]).start()

    for r in range(tiles):
        part = slice(r * ROW_TILE, (r + 1) * ROW_TILE)
        new = lax.dot_general(
            tile[:, part], tile[...], (((0,), (0,)), ((), ())),
            preferred_element_type=jnp.float32,
        )
        gram_r[part, :] = (new / width).astype(jnp.bfloat16)

    def finish(c):
        wait_bytes(r4[c].at[pl.ds(0, others)], s["x4_recv"].at[c])
        move(out.at[:, :, cols(c)], 0, r4[c], HOME_SLOT, 0, n_dp)

    last = None
    for c in order:
        wait_bytes(h3[c], s["b_recv"].at[c])
        send_ten(c, q4, r4, h3, BY_SLOT, "x4_send", "x4_recv")
        if last is not None:
            finish(last)
        last = c
    finish(last)
    wait_bytes(u_home, s["h_recv"].at[0])
    move(out.at[:, :, direct], 0, u_home, DP_OF, 0, n_dp)

    for c in range(nc):
        wait_bytes(p1[c].at[pl.ds(0, others)], s["x1_send"].at[c])
        wait_bytes(p2[c].at[pl.ds(0, n_dp - 1)], s["z_send"].at[c])
        wait_bytes(h3[c].at[pl.ds(0, n_dp - 1)], s["b_send"].at[c])
        wait_bytes(q4[c].at[pl.ds(0, others)], s["x4_send"].at[c])
    wait_bytes(d_out.at[pl.ds(0, n_dp - 1)], s["d_send"].at[0])
    wait_bytes(u_out.at[pl.ds(0, n_dp - 1)], s["h_send"].at[0])
    wait_bytes(d_all.at[pl.ds(0, n_ten - 1)], s["e_send"].at[0])
    wait_bytes(u_all.at[pl.ds(0, n_ten - 1)], s["f_send"].at[0])


def write_kernel(parts, gram_l, gram_r, update, left_out, right_out, update_out, sem):
    copies = []
    for i, (src, dst) in enumerate(((gram_l, left_out), (gram_r, right_out), (update, update_out))):
        step = src.shape[0] // parts
        for p in range(parts):
            part = slice(p * step, (p + 1) * step)
            copies.append(pltpu.make_async_copy(src.at[part], dst.at[part], sem.at[i, p]))
    for copy in copies:
        copy.start()
    for copy in copies:
        copy.wait()


def shards(gradient, owner, left_root, right_root):
    n_dp = lax.axis_size("dp")
    n_ten = lax.axis_size("tensor")
    my_ten = lax.axis_index("tensor")
    rows, width = gradient.shape[2:]
    nc = len(CHUNKS)
    idx = plan(owner, my_ten, n_dp, n_ten)
    bf16 = jnp.bfloat16

    scratch = {}
    for kind in ("g_in", "p1", "a1", "p2", "h3", "q4", "r4"):
        for c in range(nc):
            scratch[f"{kind}{c}"] = pltpu.VMEM((n_dp, rows, CHUNKS[c]), bf16)
    for kind in ("tile", "left_v", "right_v", "mixed", "upd"):
        scratch[kind] = pltpu.VMEM((width, width), bf16)
    scratch["prod"] = pltpu.VMEM((width, width), jnp.float32)
    for kind in ("d_in", "d_out", "d_block", "u_out", "u_home"):
        scratch[kind] = pltpu.VMEM((n_dp, rows, DIRECT), bf16)
    for kind in ("d_all", "u_all"):
        scratch[kind] = pltpu.VMEM((n_ten, n_dp, rows, DIRECT), bf16)
    for kind in ("x1", "z", "b", "x4"):
        for way in ("send", "recv"):
            scratch[f"{kind}_{way}"] = pltpu.SemaphoreType.DMA((nc,))
    for kind in ("d", "e", "f", "h"):
        for way in ("send", "recv"):
            scratch[f"{kind}_{way}"] = pltpu.SemaphoreType.DMA((1,))
    scratch["load_sem"] = pltpu.SemaphoreType.DMA((nc + 3,))

    any_spec = pl.BlockSpec(memory_space=pl.ANY)
    vmem_spec = pl.BlockSpec(memory_space=pltpu.VMEM)
    square = (width, width)
    strips = (n_dp, rows, width)
    held = pl.pallas_call(
        functools.partial(step_kernel, n_dp, n_ten, tuple(scratch)),
        out_shape=(pltpu.VMEM(square, bf16), pltpu.VMEM(square, bf16), pltpu.VMEM(strips, bf16)),
        in_specs=[pl.BlockSpec(memory_space=pltpu.SMEM), any_spec, any_spec, any_spec],
        out_specs=(vmem_spec, vmem_spec, vmem_spec),
        scratch_shapes=list(scratch.values()),
        compiler_params=pltpu.CompilerParams(
            collective_id=0, has_side_effects=True, vmem_limit_bytes=46 << 20
        ),
        name="shampoo_step",
    )(idx, gradient.reshape(strips), left_root[0], right_root[0])
    parts = 4
    left_new, right_new, update = pl.pallas_call(
        functools.partial(write_kernel, parts),
        out_shape=(
            jax.ShapeDtypeStruct(square, bf16),
            jax.ShapeDtypeStruct(square, bf16),
            jax.ShapeDtypeStruct(strips, bf16),
        ),
        in_specs=[vmem_spec] * 3,
        out_specs=(any_spec,) * 3,
        scratch_shapes=[pltpu.SemaphoreType.DMA((3, parts))],
        compiler_params=pltpu.CompilerParams(vmem_limit_bytes=1 << 20),
        name="write_results",
    )(*(pltpu.with_memory_space_constraint(x, pltpu.VMEM) for x in held))
    return left_new[None], right_new[None], update.reshape(gradient.shape)


def solution(mesh):
    return jax.shard_map(
        shards,
        mesh=mesh,
        in_specs=(
            P(None, "tensor", "dp", None),
            P(),
            P(("dp", "tensor"), None, None),
            P(("dp", "tensor"), None, None),
        ),
        out_specs=(
            P(("dp", "tensor"), None, None),
            P(("dp", "tensor"), None, None),
            P(None, "tensor", "dp", None),
        ),
        check_vma=False,
    )
```

```python
import functools

import jax
import jax.numpy as jnp
from jax import lax
from jax.experimental import pallas as pl
from jax.experimental.pallas import tpu as pltpu
from jax.sharding import PartitionSpec as P

MESH = pl.DeviceIdType.MESH
DIRECT = 128
CHUNKS = (128, 256, 256, 256)
STARTS = tuple(DIRECT + sum(CHUNKS[:c]) for c in range(len(CHUNKS)))
ROW_TILE = 256
LANES = 128
OUT_ORDER, BY_DP, BY_SLOT, HOME_SLOT, AT_DP, DP_OF, SLAB_OF, TEN_OF = range(8)


def fill_plan(owner, table, my_ten, n_dp, n_ten):
    group = n_dp // n_ten
    square = (n_dp, n_dp)
    row = lax.broadcasted_iota(jnp.int32, square, 0)
    lane = lax.broadcasted_iota(jnp.int32, square, 1)

    def column(where, values):
        return jnp.sum(jnp.where(where, values, 0), axis=1, keepdims=True)

    zero = jnp.zeros((n_dp, 1), jnp.int32)
    by_dp, by_slot, slab_of = zero, zero, zero
    home_slot = dp_of = ten_of = jnp.zeros((1, n_dp), jnp.int32)
    for t in range(n_ten):
        first = t * n_dp
        line, start = first // LANES, first % LANES
        own = owner[line:line + 1, start:start + n_dp]
        ten = jnp.bitwise_and(own, n_ten - 1)
        dp = lax.shift_right_logical(own, n_ten.bit_length() - 1)
        same = column(row == lane, ten) == ten
        rank = jnp.sum(jnp.where(same & (row < lane), 1, 0), axis=0, keepdims=True)
        slot = t * group + rank
        mine = ten == my_ten
        at_dp = mine & (dp == row)
        by_dp += column(at_dp, slot)
        slab_of += column(at_dp, t)
        by_slot += column(mine & (slot == row), dp)
        here = jnp.where(my_ten == t, 1, 0)
        home_slot += here * (ten * group + rank)
        dp_of += here * dp
        ten_of += here * ten
    columns = {
        OUT_ORDER: column(home_slot == row, lane),
        BY_DP: by_dp,
        BY_SLOT: by_slot,
        HOME_SLOT: column(row == lane, home_slot),
        AT_DP: column(dp_of == row, lane),
        DP_OF: column(row == lane, dp_of),
        SLAB_OF: jnp.bitwise_and(slab_of, n_ten - 1),
        TEN_OF: jnp.bitwise_and(column(dp_of == row, ten_of), n_ten - 1),
    }
    which = lax.broadcasted_iota(jnp.int32, table.shape, 1)
    full = jnp.zeros(table.shape, jnp.int32)
    for place, values in columns.items():
        full = jnp.where(which == place, values, full)
    table[...] = jnp.bitwise_and(full, n_dp - 1)


def step_kernel(n_dp, n_ten, names, owner, grad, left_root, right_root, gram_l, gram_r, out, *scratch):
    s = dict(zip(names, scratch, strict=True))
    nc = len(CHUNKS)
    g_in, p1, a1, p2, h3, q4, r4 = (
        [s[f"{kind}{c}"] for c in range(nc)] for kind in ("g_in", "p1", "a1", "p2", "h3", "q4", "r4")
    )
    tile, left_v, right_v, mixed, prod, upd = (
        s[k] for k in ("tile", "left_v", "right_v", "mixed", "prod", "upd")
    )
    d_in, d_out, d_block, d_all, u_all, u_out, u_home = (
        s[k] for k in ("d_in", "d_out", "d_block", "d_all", "u_all", "u_out", "u_home")
    )
    load_sem = s["load_sem"]
    group = n_dp // n_ten
    rows, width = grad.shape[1], grad.shape[2]
    me = lax.axis_index("dp")
    my_ten = lax.axis_index("tensor")
    core = lax.rem(me, 2)
    chip = me // 2
    n_chip = n_dp // 2
    direct = slice(0, DIRECT)

    def cols(c):
        return slice(STARTS[c], STARTS[c] + CHUNKS[c])

    barrier = pltpu.get_barrier_semaphore()

    def greet_dp(k, carry):
        pl.semaphore_signal(
            barrier, inc=1, device_id=(lax.rem(me + k, n_dp), my_ten), device_id_type=MESH
        )
        return carry

    def greet_ten(k, carry):
        pl.semaphore_signal(
            barrier, inc=1, device_id=(me, lax.rem(my_ten + k, n_ten)), device_id_type=MESH
        )
        return carry

    lax.fori_loop(1, n_ten, greet_ten, 0)
    lax.fori_loop(1, n_dp, greet_dp, 0)

    idx = s["idx"]
    load_owner = pltpu.make_async_copy(owner, s["owner_v"], load_sem.at[nc + 3])
    load_owner.start()
    load_direct = pltpu.make_async_copy(grad.at[:, :, direct], d_in, load_sem.at[nc])
    loads = [
        pltpu.make_async_copy(grad.at[:, :, cols(c)], g_in[c], load_sem.at[c]) for c in range(nc)
    ]
    load_right = pltpu.make_async_copy(right_root, right_v, load_sem.at[nc + 1])
    load_left = pltpu.make_async_copy(left_root, left_v, load_sem.at[nc + 2])
    for copy in (load_direct, *loads, load_right, load_left):
        copy.start()

    def move(dst, dst_base, src, which, idx_base, count):
        def body(j, carry):
            dst[dst_base + j] = src[idx[idx_base + j, which]]
            return carry

        lax.fori_loop(0, count, body, 0, unroll=8)

    def wait_bytes(ref, sem):
        pltpu.make_async_copy(ref, ref, sem).wait()

    def strip_rows(d):
        return pl.ds(pl.multiple_of(d * rows, rows), rows)

    others = (n_ten - 1) * group

    def ten_copy(c, k, src, dst, send, recv):
        to = lax.rem(my_ten + k, n_ten)
        return pltpu.make_async_remote_copy(
            src_ref=src[c].at[pl.ds(to * group, group)],
            dst_ref=dst[c].at[pl.ds(my_ten * group, group)],
            send_sem=s[send].at[c],
            recv_sem=s[recv].at[c],
            device_id=(me, to),
            device_id_type=MESH,
        )

    def send_ten(c, packed, arrived, src, which, send, recv):
        for k in (2, 1, 3):
            to = lax.rem(my_ten + k, n_ten)
            move(packed[c], to * group, src[c], which, to * group, group)
            ten_copy(c, k, packed, arrived, send, recv).start()
        move(arrived[c], my_ten * group, src[c], which, my_ten * group, group)

    def send_whole(src, dst, send, recv):
        for k in (2, 1, 3):
            pltpu.make_async_remote_copy(
                src_ref=src,
                dst_ref=dst.at[my_ten],
                send_sem=s[send].at[0],
                recv_sem=s[recv].at[0],
                device_id=(me, lax.rem(my_ten + k, n_ten)),
                device_id_type=MESH,
            ).start()

    def send_class(copy, local, k):
        def body(i, carry):
            copy(lax.rem(chip + i, n_chip) * 2 + k).start()
            return carry

        lax.fori_loop(1, n_chip, body, 0)

        @pl.when(core != k)
        def _():
            copy(chip * 2 + k).start()

        @pl.when(core == k)
        def _():
            local().start()

    def dp_copy(src, dst, send, recv, to):
        return pltpu.make_async_remote_copy(
            src_ref=src, dst_ref=dst, send_sem=send, recv_sem=recv,
            device_id=(to, my_ten), device_id_type=MESH,
        )

    def forward_direct(to):
        return dp_copy(d_out.at[to], d_block.at[me], s["d_send"].at[0], s["d_recv"].at[0], to)

    def forward_direct_local():
        return pltpu.make_async_copy(d_out.at[me], d_block.at[me], s["d_recv"].at[0])

    def forward(c, to):
        return dp_copy(
            p2[c].at[to], tile.at[strip_rows(me), cols(c)], s["z_send"].at[c], s["z_recv"].at[c], to
        )

    def forward_local(c):
        return pltpu.make_async_copy(
            p2[c].at[me], tile.at[strip_rows(me), cols(c)], s["z_recv"].at[c]
        )

    load_owner.wait()
    fill_plan(s["owner_v"], s["table"], my_ten, n_dp, n_ten)
    keep_plan = pltpu.make_async_copy(s["table"], idx, load_sem.at[nc + 3])
    keep_plan.start()
    keep_plan.wait()
    load_direct.wait()
    move(d_out, 0, d_in, AT_DP, 0, n_dp)
    loads[0].wait()
    pl.semaphore_wait(barrier, n_dp + n_ten - 2)
    for k in range(2):
        send_class(forward_direct, forward_direct_local, k)
    for c in range(nc):
        if c > 0:
            loads[c].wait()
        send_ten(c, p1, a1, g_in, OUT_ORDER, "x1_send", "x1_recv")

    for c in range(nc):
        wait_bytes(a1[c].at[pl.ds(0, others)], s["x1_recv"].at[c])
        move(p2[c], 0, a1[c], BY_DP, 0, n_dp)
        send_class(functools.partial(forward, c), functools.partial(forward_local, c), 0)
    for c in range(nc):
        send_class(functools.partial(forward, c), functools.partial(forward_local, c), 1)

    wait_bytes(d_block, s["d_recv"].at[0])
    send_whole(d_block, d_all, "e_send", "e_recv")

    def keep(i, carry):
        d_all[my_ten, i] = d_block[i]
        return carry

    lax.fori_loop(0, n_dp, keep, 0, unroll=8)
    wait_bytes(d_all.at[pl.ds(0, n_ten - 1)], s["e_recv"].at[0])
    slab = idx[me, SLAB_OF]

    def take(i, carry):
        tile[strip_rows(i), direct] = d_all[slab, i]
        return carry

    lax.fori_loop(0, n_dp, take, 0, unroll=8)

    load_right.wait()
    load_left.wait()
    for c in range(nc):
        wait_bytes(tile.at[:, cols(c)], s["z_recv"].at[c])

    tiles = width // ROW_TILE

    def row_tile(r):
        return pl.ds(pl.multiple_of(r * ROW_TILE, ROW_TILE), ROW_TILE)

    def mix(r, total):
        g = tile[row_tile(r), :]
        mixed[row_tile(r), :] = jnp.dot(
            g, right_v[...], preferred_element_type=jnp.float32
        ).astype(jnp.bfloat16)
        g = g.astype(jnp.float32)
        return total + jnp.sum(g * g, axis=0, keepdims=True)

    def precondition(r, total):
        p = jnp.dot(left_v[row_tile(r), :], mixed[...], preferred_element_type=jnp.float32)
        prod[row_tile(r), :] = p
        return total + jnp.sum(p * p, axis=0, keepdims=True)

    zero = jnp.zeros((1, width), jnp.float32)
    grad_sum = lax.fori_loop(0, tiles, mix, zero)
    prod_sum = lax.fori_loop(0, tiles, precondition, zero)
    entries = width * width
    grad_sq = jnp.sum(grad_sum, axis=1, keepdims=True) / entries
    prod_sq = jnp.sum(prod_sum, axis=1, keepdims=True) / entries
    scale = jnp.sqrt(grad_sq) / jnp.sqrt(prod_sq + 1e-06)

    def graft(r, carry):
        upd[row_tile(r), :] = (prod[row_tile(r), :] * scale).astype(jnp.bfloat16)
        return carry

    lax.fori_loop(0, tiles, graft, 0)

    def keep_update(i, carry):
        u_all[my_ten, i] = upd[strip_rows(i), direct]
        return carry

    lax.fori_loop(0, n_dp, keep_update, 0, unroll=8)
    send_whole(u_all.at[my_ten], u_all, "f_send", "f_recv")

    order = range(nc - 1, -1, -1)
    for c in order:

        def send_back(i, carry, c=c):
            to = lax.rem(me + i, n_dp)
            dp_copy(
                upd.at[strip_rows(to), cols(c)], h3[c].at[me],
                s["b_send"].at[c], s["b_recv"].at[c], to,
            ).start()
            return carry

        lax.fori_loop(1, n_dp, send_back, 0)
        pltpu.make_async_copy(
            upd.at[strip_rows(me), cols(c)], h3[c].at[me], s["b_recv"].at[c]
        ).start()

    def left_stat(r, carry):
        new = lax.dot_general(
            tile[row_tile(r), :], tile[...], (((1,), (1,)), ((), ())),
            preferred_element_type=jnp.float32,
        )
        gram_l[row_tile(r), :] = (new / width).astype(jnp.bfloat16)
        return carry

    lax.fori_loop(0, tiles, left_stat, 0)

    wait_bytes(u_all.at[pl.ds(0, n_ten - 1)], s["f_recv"].at[0])
    ten = idx[me, TEN_OF]

    def take_update(i, carry):
        u_out[i] = u_all[ten, i]
        return carry

    lax.fori_loop(0, n_dp, take_update, 0, unroll=8)

    def send_home(i, carry):
        to = lax.rem(me + i, n_dp)
        dp_copy(u_out.at[to], u_home.at[me], s["h_send"].at[0], s["h_recv"].at[0], to).start()
        return carry

    lax.fori_loop(1, n_dp, send_home, 0)
    pltpu.make_async_copy(u_out.at[me], u_home.at[me], s["h_recv"].at[0]).start()

    for r in range(tiles):
        part = slice(r * ROW_TILE, (r + 1) * ROW_TILE)
        new = lax.dot_general(
            tile[:, part], tile[...], (((0,), (0,)), ((), ())),
            preferred_element_type=jnp.float32,
        )
        gram_r[part, :] = (new / width).astype(jnp.bfloat16)

    def finish(c):
        wait_bytes(r4[c].at[pl.ds(0, others)], s["x4_recv"].at[c])
        move(out.at[:, :, cols(c)], 0, r4[c], HOME_SLOT, 0, n_dp)

    last = None
    for c in order:
        wait_bytes(h3[c], s["b_recv"].at[c])
        send_ten(c, q4, r4, h3, BY_SLOT, "x4_send", "x4_recv")
        if last is not None:
            finish(last)
        last = c
    finish(last)
    wait_bytes(u_home, s["h_recv"].at[0])
    move(out.at[:, :, direct], 0, u_home, DP_OF, 0, n_dp)

    for c in range(nc):
        wait_bytes(p1[c].at[pl.ds(0, others)], s["x1_send"].at[c])
        wait_bytes(p2[c].at[pl.ds(0, n_dp - 1)], s["z_send"].at[c])
        wait_bytes(h3[c].at[pl.ds(0, n_dp - 1)], s["b_send"].at[c])
        wait_bytes(q4[c].at[pl.ds(0, others)], s["x4_send"].at[c])
    wait_bytes(d_out.at[pl.ds(0, n_dp - 1)], s["d_send"].at[0])
    wait_bytes(u_out.at[pl.ds(0, n_dp - 1)], s["h_send"].at[0])
    wait_bytes(d_all.at[pl.ds(0, n_ten - 1)], s["e_send"].at[0])
    wait_bytes(u_all.at[pl.ds(0, n_ten - 1)], s["f_send"].at[0])


def write_kernel(parts, gram_l, gram_r, update, left_out, right_out, update_out, sem):
    copies = []
    for i, (src, dst) in enumerate(((gram_l, left_out), (gram_r, right_out), (update, update_out))):
        step = src.shape[0] // parts
        for p in range(parts):
            part = slice(p * step, (p + 1) * step)
            copies.append(pltpu.make_async_copy(src.at[part], dst.at[part], sem.at[i, p]))
    for copy in copies:
        copy.start()
    for copy in copies:
        copy.wait()


def shards(gradient, owner, left_root, right_root):
    n_dp = lax.axis_size("dp")
    n_ten = lax.axis_size("tensor")
    rows, width = gradient.shape[2:]
    nc = len(CHUNKS)
    bf16 = jnp.bfloat16

    scratch = {}
    for kind in ("g_in", "p1", "a1", "p2", "h3", "q4", "r4"):
        for c in range(nc):
            scratch[f"{kind}{c}"] = pltpu.VMEM((n_dp, rows, CHUNKS[c]), bf16)
    for kind in ("tile", "left_v", "right_v", "mixed", "upd"):
        scratch[kind] = pltpu.VMEM((width, width), bf16)
    scratch["prod"] = pltpu.VMEM((width, width), jnp.float32)
    for kind in ("d_in", "d_out", "d_block", "u_out", "u_home"):
        scratch[kind] = pltpu.VMEM((n_dp, rows, DIRECT), bf16)
    for kind in ("d_all", "u_all"):
        scratch[kind] = pltpu.VMEM((n_ten, n_dp, rows, DIRECT), bf16)
    for kind in ("x1", "z", "b", "x4"):
        for way in ("send", "recv"):
            scratch[f"{kind}_{way}"] = pltpu.SemaphoreType.DMA((nc,))
    for kind in ("d", "e", "f", "h"):
        for way in ("send", "recv"):
            scratch[f"{kind}_{way}"] = pltpu.SemaphoreType.DMA((1,))
    scratch["load_sem"] = pltpu.SemaphoreType.DMA((nc + 4,))
    scratch["owner_v"] = pltpu.VMEM((n_ten * n_dp // LANES, LANES), jnp.int32)
    scratch["table"] = pltpu.VMEM((n_dp, LANES), jnp.int32)
    scratch["idx"] = pltpu.SMEM((n_dp, LANES), jnp.int32)

    any_spec = pl.BlockSpec(memory_space=pl.ANY)
    vmem_spec = pl.BlockSpec(memory_space=pltpu.VMEM)
    square = (width, width)
    strips = (n_dp, rows, width)
    held = pl.pallas_call(
        functools.partial(step_kernel, n_dp, n_ten, tuple(scratch)),
        out_shape=(pltpu.VMEM(square, bf16), pltpu.VMEM(square, bf16), pltpu.VMEM(strips, bf16)),
        in_specs=[any_spec] * 4,
        out_specs=(vmem_spec, vmem_spec, vmem_spec),
        scratch_shapes=list(scratch.values()),
        compiler_params=pltpu.CompilerParams(
            collective_id=0, has_side_effects=True, vmem_limit_bytes=46 << 20
        ),
        name="shampoo_step",
    )(owner.reshape(-1, LANES), gradient.reshape(strips), left_root[0], right_root[0])
    parts = 4
    left_new, right_new, update = pl.pallas_call(
        functools.partial(write_kernel, parts),
        out_shape=(
            jax.ShapeDtypeStruct(square, bf16),
            jax.ShapeDtypeStruct(square, bf16),
            jax.ShapeDtypeStruct(strips, bf16),
        ),
        in_specs=[vmem_spec] * 3,
        out_specs=(any_spec,) * 3,
        scratch_shapes=[pltpu.SemaphoreType.DMA((3, parts))],
        compiler_params=pltpu.CompilerParams(vmem_limit_bytes=1 << 20),
        name="write_results",
    )(*(pltpu.with_memory_space_constraint(x, pltpu.VMEM) for x in held))
    return left_new[None], right_new[None], update.reshape(gradient.shape)


def solution(mesh):
    return jax.shard_map(
        shards,
        mesh=mesh,
        in_specs=(
            P(None, "tensor", "dp", None),
            P(),
            P(("dp", "tensor"), None, None),
            P(("dp", "tensor"), None, None),
        ),
        out_specs=(
            P(("dp", "tensor"), None, None),
            P(("dp", "tensor"), None, None),
            P(None, "tensor", "dp", None),
        ),
        check_vma=False,
    )
```

```python
import functools

import jax
import jax.numpy as jnp
from jax import lax
from jax.experimental import pallas as pl
from jax.experimental.pallas import tpu as pltpu
from jax.sharding import PartitionSpec as P

MESH = pl.DeviceIdType.MESH
DIRECT = 128
CHUNKS = (128, 256, 256, 256)
STARTS = tuple(DIRECT + sum(CHUNKS[:c]) for c in range(len(CHUNKS)))
BOTH = 1
ROW_TILE = 256
LANES = 128
OUT_ORDER, BY_DP, BY_SLOT, HOME_SLOT, AT_DP, DP_OF, SLAB_OF, TEN_OF = range(8)


def fill_plan(owner, table, my_ten, n_dp, n_ten):
    group = n_dp // n_ten
    square = (n_dp, n_dp)
    row = lax.broadcasted_iota(jnp.int32, square, 0)
    lane = lax.broadcasted_iota(jnp.int32, square, 1)

    def column(where, values):
        return jnp.sum(jnp.where(where, values, 0), axis=1, keepdims=True)

    zero = jnp.zeros((n_dp, 1), jnp.int32)
    by_dp, by_slot, slab_of = zero, zero, zero
    home_slot = dp_of = ten_of = jnp.zeros((1, n_dp), jnp.int32)
    for t in range(n_ten):
        first = t * n_dp
        line, start = first // LANES, first % LANES
        own = owner[line:line + 1, start:start + n_dp]
        ten = jnp.bitwise_and(own, n_ten - 1)
        dp = lax.shift_right_logical(own, n_ten.bit_length() - 1)
        same = column(row == lane, ten) == ten
        rank = jnp.sum(jnp.where(same & (row < lane), 1, 0), axis=0, keepdims=True)
        slot = t * group + rank
        mine = ten == my_ten
        at_dp = mine & (dp == row)
        by_dp += column(at_dp, slot)
        slab_of += column(at_dp, t)
        by_slot += column(mine & (slot == row), dp)
        here = jnp.where(my_ten == t, 1, 0)
        home_slot += here * (ten * group + rank)
        dp_of += here * dp
        ten_of += here * ten
    columns = {
        OUT_ORDER: column(home_slot == row, lane),
        BY_DP: by_dp,
        BY_SLOT: by_slot,
        HOME_SLOT: column(row == lane, home_slot),
        AT_DP: column(dp_of == row, lane),
        DP_OF: column(row == lane, dp_of),
        SLAB_OF: jnp.bitwise_and(slab_of, n_ten - 1),
        TEN_OF: jnp.bitwise_and(column(dp_of == row, ten_of), n_ten - 1),
    }
    which = lax.broadcasted_iota(jnp.int32, table.shape, 1)
    full = jnp.zeros(table.shape, jnp.int32)
    for place, values in columns.items():
        full = jnp.where(which == place, values, full)
    table[...] = jnp.bitwise_and(full, n_dp - 1)


def step_kernel(n_dp, n_ten, names, owner, grad, left_root, right_root, gram_l, gram_r, out, *scratch):
    s = dict(zip(names, scratch, strict=True))
    nc = len(CHUNKS)
    g_in, p1, a1, p2, h3, q4, r4 = (
        [s[f"{kind}{c}"] for c in range(nc)] for kind in ("g_in", "p1", "a1", "p2", "h3", "q4", "r4")
    )
    tile, left_v, right_v, mixed, prod, upd = (
        s[k] for k in ("tile", "left_v", "right_v", "mixed", "prod", "upd")
    )
    d_in, d_out, d_block, d_all, u_all, u_out, u_home = (
        s[k] for k in ("d_in", "d_out", "d_block", "d_all", "u_all", "u_out", "u_home")
    )
    load_sem = s["load_sem"]
    group = n_dp // n_ten
    rows, width = grad.shape[1], grad.shape[2]
    me = lax.axis_index("dp")
    my_ten = lax.axis_index("tensor")
    core = lax.rem(me, 2)
    chip = me // 2
    n_chip = n_dp // 2
    direct = slice(0, DIRECT)

    def cols(c):
        return slice(STARTS[c], STARTS[c] + CHUNKS[c])

    barrier = pltpu.get_barrier_semaphore()

    def greet_dp(k, carry):
        pl.semaphore_signal(
            barrier, inc=1, device_id=(lax.rem(me + k, n_dp), my_ten), device_id_type=MESH
        )
        return carry

    def greet_ten(k, carry):
        pl.semaphore_signal(
            barrier, inc=1, device_id=(me, lax.rem(my_ten + k, n_ten)), device_id_type=MESH
        )
        return carry

    lax.fori_loop(1, n_ten, greet_ten, 0)
    lax.fori_loop(1, n_dp, greet_dp, 0)

    idx = s["idx"]
    load_owner = pltpu.make_async_copy(owner, s["owner_v"], load_sem.at[nc + 3])
    load_owner.start()
    load_direct = pltpu.make_async_copy(grad.at[:, :, direct], d_in, load_sem.at[nc])
    loads = [
        pltpu.make_async_copy(grad.at[:, :, cols(c)], g_in[c], load_sem.at[c]) for c in range(nc)
    ]
    load_right = pltpu.make_async_copy(right_root, right_v, load_sem.at[nc + 1])
    load_left = pltpu.make_async_copy(left_root, left_v, load_sem.at[nc + 2])
    for copy in (load_direct, *loads, load_right, load_left):
        copy.start()

    def move(dst, dst_base, src, which, idx_base, count):
        def body(j, carry):
            dst[dst_base + j] = src[idx[idx_base + j, which]]
            return carry

        lax.fori_loop(0, count, body, 0, unroll=8)

    def wait_bytes(ref, sem):
        pltpu.make_async_copy(ref, ref, sem).wait()

    def strip_rows(d):
        return pl.ds(pl.multiple_of(d * rows, rows), rows)

    others = (n_ten - 1) * group

    def ten_copy(c, k, src, dst, send, recv):
        to = lax.rem(my_ten + k, n_ten)
        return pltpu.make_async_remote_copy(
            src_ref=src[c].at[pl.ds(to * group, group)],
            dst_ref=dst[c].at[pl.ds(my_ten * group, group)],
            send_sem=s[send].at[c],
            recv_sem=s[recv].at[c],
            device_id=(me, to),
            device_id_type=MESH,
        )

    def send_ten(c, packed, arrived, src, which, send, recv):
        for k in (2, 1, 3):
            to = lax.rem(my_ten + k, n_ten)
            move(packed[c], to * group, src[c], which, to * group, group)
            ten_copy(c, k, packed, arrived, send, recv).start()
        move(arrived[c], my_ten * group, src[c], which, my_ten * group, group)

    def send_whole(src, dst, send, recv):
        for k in (2, 1, 3):
            pltpu.make_async_remote_copy(
                src_ref=src,
                dst_ref=dst.at[my_ten],
                send_sem=s[send].at[0],
                recv_sem=s[recv].at[0],
                device_id=(me, lax.rem(my_ten + k, n_ten)),
                device_id_type=MESH,
            ).start()

    def send_class(copy, local, k):
        def body(i, carry):
            copy(lax.rem(chip + i, n_chip) * 2 + k).start()
            return carry

        lax.fori_loop(1, n_chip, body, 0)

        @pl.when(core != k)
        def _():
            copy(chip * 2 + k).start()

        @pl.when(core == k)
        def _():
            local().start()

    def dp_copy(src, dst, send, recv, to):
        return pltpu.make_async_remote_copy(
            src_ref=src, dst_ref=dst, send_sem=send, recv_sem=recv,
            device_id=(to, my_ten), device_id_type=MESH,
        )

    def forward_direct(to):
        return dp_copy(d_out.at[to], d_block.at[me], s["d_send"].at[0], s["d_recv"].at[0], to)

    def forward_direct_local():
        return pltpu.make_async_copy(d_out.at[me], d_block.at[me], s["d_recv"].at[0])

    def forward(c, to):
        return dp_copy(
            p2[c].at[to], tile.at[strip_rows(me), cols(c)], s["z_send"].at[c], s["z_recv"].at[c], to
        )

    def forward_local(c):
        return pltpu.make_async_copy(
            p2[c].at[me], tile.at[strip_rows(me), cols(c)], s["z_recv"].at[c]
        )

    load_owner.wait()
    fill_plan(s["owner_v"], s["table"], my_ten, n_dp, n_ten)
    keep_plan = pltpu.make_async_copy(s["table"], idx, load_sem.at[nc + 3])
    keep_plan.start()
    keep_plan.wait()
    load_direct.wait()
    move(d_out, 0, d_in, AT_DP, 0, n_dp)
    loads[0].wait()
    pl.semaphore_wait(barrier, n_dp + n_ten - 2)
    for k in range(2):
        send_class(forward_direct, forward_direct_local, k)
    for c in range(nc):
        if c > 0:
            loads[c].wait()
        send_ten(c, p1, a1, g_in, OUT_ORDER, "x1_send", "x1_recv")

    for c in range(nc):
        wait_bytes(a1[c].at[pl.ds(0, others)], s["x1_recv"].at[c])
        move(p2[c], 0, a1[c], BY_DP, 0, n_dp)
        send_class(functools.partial(forward, c), functools.partial(forward_local, c), 0)
        if c < BOTH:
            send_class(functools.partial(forward, c), functools.partial(forward_local, c), 1)
    for c in range(BOTH, nc):
        send_class(functools.partial(forward, c), functools.partial(forward_local, c), 1)

    wait_bytes(d_block, s["d_recv"].at[0])
    send_whole(d_block, d_all, "e_send", "e_recv")

    def keep(i, carry):
        d_all[my_ten, i] = d_block[i]
        return carry

    lax.fori_loop(0, n_dp, keep, 0, unroll=8)
    wait_bytes(d_all.at[pl.ds(0, n_ten - 1)], s["e_recv"].at[0])
    slab = idx[me, SLAB_OF]

    def take(i, carry):
        tile[strip_rows(i), direct] = d_all[slab, i]
        return carry

    lax.fori_loop(0, n_dp, take, 0, unroll=8)

    load_right.wait()
    load_left.wait()
    for c in range(nc):
        wait_bytes(tile.at[:, cols(c)], s["z_recv"].at[c])

    tiles = width // ROW_TILE

    def row_tile(r):
        return pl.ds(pl.multiple_of(r * ROW_TILE, ROW_TILE), ROW_TILE)

    def mix(r, total):
        g = tile[row_tile(r), :]
        mixed[row_tile(r), :] = jnp.dot(
            g, right_v[...], preferred_element_type=jnp.float32
        ).astype(jnp.bfloat16)
        g = g.astype(jnp.float32)
        return total + jnp.sum(g * g, axis=0, keepdims=True)

    def precondition(r, total):
        p = jnp.dot(left_v[row_tile(r), :], mixed[...], preferred_element_type=jnp.float32)
        prod[row_tile(r), :] = p
        return total + jnp.sum(p * p, axis=0, keepdims=True)

    zero = jnp.zeros((1, width), jnp.float32)
    grad_sum = lax.fori_loop(0, tiles, mix, zero)
    prod_sum = lax.fori_loop(0, tiles, precondition, zero)
    entries = width * width
    grad_sq = jnp.sum(grad_sum, axis=1, keepdims=True) / entries
    prod_sq = jnp.sum(prod_sum, axis=1, keepdims=True) / entries
    scale = jnp.sqrt(grad_sq) / jnp.sqrt(prod_sq + 1e-06)

    def graft(r, carry):
        upd[row_tile(r), :] = (prod[row_tile(r), :] * scale).astype(jnp.bfloat16)
        return carry

    lax.fori_loop(0, tiles, graft, 0)

    def keep_update(i, carry):
        u_all[my_ten, i] = upd[strip_rows(i), direct]
        return carry

    lax.fori_loop(0, n_dp, keep_update, 0, unroll=8)
    send_whole(u_all.at[my_ten], u_all, "f_send", "f_recv")

    order = range(nc - 1, -1, -1)
    for c in order:

        def send_back(i, carry, c=c):
            to = lax.rem(me + i, n_dp)
            dp_copy(
                upd.at[strip_rows(to), cols(c)], h3[c].at[me],
                s["b_send"].at[c], s["b_recv"].at[c], to,
            ).start()
            return carry

        lax.fori_loop(1, n_dp, send_back, 0)
        pltpu.make_async_copy(
            upd.at[strip_rows(me), cols(c)], h3[c].at[me], s["b_recv"].at[c]
        ).start()

    def left_stat(r, carry):
        new = lax.dot_general(
            tile[row_tile(r), :], tile[...], (((1,), (1,)), ((), ())),
            preferred_element_type=jnp.float32,
        )
        gram_l[row_tile(r), :] = (new / width).astype(jnp.bfloat16)
        return carry

    lax.fori_loop(0, tiles, left_stat, 0)

    wait_bytes(u_all.at[pl.ds(0, n_ten - 1)], s["f_recv"].at[0])
    ten = idx[me, TEN_OF]

    def take_update(i, carry):
        u_out[i] = u_all[ten, i]
        return carry

    lax.fori_loop(0, n_dp, take_update, 0, unroll=8)

    def send_home():
        def body(i, carry):
            to = lax.rem(me + i, n_dp)
            dp_copy(u_out.at[to], u_home.at[me], s["h_send"].at[0], s["h_recv"].at[0], to).start()
            return carry

        lax.fori_loop(1, n_dp, body, 0)
        pltpu.make_async_copy(u_out.at[me], u_home.at[me], s["h_recv"].at[0]).start()

    pl.when(core == 1)(send_home)

    for r in range(tiles):
        part = slice(r * ROW_TILE, (r + 1) * ROW_TILE)
        new = lax.dot_general(
            tile[:, part], tile[...], (((0,), (0,)), ((), ())),
            preferred_element_type=jnp.float32,
        )
        gram_r[part, :] = (new / width).astype(jnp.bfloat16)

    def finish(c):
        wait_bytes(r4[c].at[pl.ds(0, others)], s["x4_recv"].at[c])
        move(out.at[:, :, cols(c)], 0, r4[c], HOME_SLOT, 0, n_dp)

    last = None
    for c in order:
        wait_bytes(h3[c], s["b_recv"].at[c])
        send_ten(c, q4, r4, h3, BY_SLOT, "x4_send", "x4_recv")
        if c == order[-2]:
            pl.when(core == 0)(send_home)
        if last is not None:
            finish(last)
        last = c
    finish(last)
    wait_bytes(u_home, s["h_recv"].at[0])
    move(out.at[:, :, direct], 0, u_home, DP_OF, 0, n_dp)

    for c in range(nc):
        wait_bytes(p1[c].at[pl.ds(0, others)], s["x1_send"].at[c])
        wait_bytes(p2[c].at[pl.ds(0, n_dp - 1)], s["z_send"].at[c])
        wait_bytes(h3[c].at[pl.ds(0, n_dp - 1)], s["b_send"].at[c])
        wait_bytes(q4[c].at[pl.ds(0, others)], s["x4_send"].at[c])
    wait_bytes(d_out.at[pl.ds(0, n_dp - 1)], s["d_send"].at[0])
    wait_bytes(u_out.at[pl.ds(0, n_dp - 1)], s["h_send"].at[0])
    wait_bytes(d_all.at[pl.ds(0, n_ten - 1)], s["e_send"].at[0])
    wait_bytes(u_all.at[pl.ds(0, n_ten - 1)], s["f_send"].at[0])


def write_kernel(parts, gram_l, gram_r, update, left_out, right_out, update_out, sem):
    copies = []
    for i, (src, dst) in enumerate(((gram_l, left_out), (gram_r, right_out), (update, update_out))):
        step = src.shape[0] // parts
        for p in range(parts):
            part = slice(p * step, (p + 1) * step)
            copies.append(pltpu.make_async_copy(src.at[part], dst.at[part], sem.at[i, p]))
    for copy in copies:
        copy.start()
    for copy in copies:
        copy.wait()


def shards(gradient, owner, left_root, right_root):
    n_dp = lax.axis_size("dp")
    n_ten = lax.axis_size("tensor")
    rows, width = gradient.shape[2:]
    nc = len(CHUNKS)
    bf16 = jnp.bfloat16

    scratch = {}
    for kind in ("g_in", "p1", "a1", "p2", "h3", "q4", "r4"):
        for c in range(nc):
            scratch[f"{kind}{c}"] = pltpu.VMEM((n_dp, rows, CHUNKS[c]), bf16)
    for kind in ("tile", "left_v", "right_v", "mixed", "upd"):
        scratch[kind] = pltpu.VMEM((width, width), bf16)
    scratch["prod"] = pltpu.VMEM((width, width), jnp.float32)
    for kind in ("d_in", "d_out", "d_block", "u_out", "u_home"):
        scratch[kind] = pltpu.VMEM((n_dp, rows, DIRECT), bf16)
    for kind in ("d_all", "u_all"):
        scratch[kind] = pltpu.VMEM((n_ten, n_dp, rows, DIRECT), bf16)
    for kind in ("x1", "z", "b", "x4"):
        for way in ("send", "recv"):
            scratch[f"{kind}_{way}"] = pltpu.SemaphoreType.DMA((nc,))
    for kind in ("d", "e", "f", "h"):
        for way in ("send", "recv"):
            scratch[f"{kind}_{way}"] = pltpu.SemaphoreType.DMA((1,))
    scratch["load_sem"] = pltpu.SemaphoreType.DMA((nc + 4,))
    scratch["owner_v"] = pltpu.VMEM((n_ten * n_dp // LANES, LANES), jnp.int32)
    scratch["table"] = pltpu.VMEM((n_dp, LANES), jnp.int32)
    scratch["idx"] = pltpu.SMEM((n_dp, LANES), jnp.int32)

    any_spec = pl.BlockSpec(memory_space=pl.ANY)
    vmem_spec = pl.BlockSpec(memory_space=pltpu.VMEM)
    square = (width, width)
    strips = (n_dp, rows, width)
    held = pl.pallas_call(
        functools.partial(step_kernel, n_dp, n_ten, tuple(scratch)),
        out_shape=(pltpu.VMEM(square, bf16), pltpu.VMEM(square, bf16), pltpu.VMEM(strips, bf16)),
        in_specs=[any_spec] * 4,
        out_specs=(vmem_spec, vmem_spec, vmem_spec),
        scratch_shapes=list(scratch.values()),
        compiler_params=pltpu.CompilerParams(
            collective_id=0, has_side_effects=True, vmem_limit_bytes=46 << 20
        ),
        name="shampoo_step",
    )(owner.reshape(-1, LANES), gradient.reshape(strips), left_root[0], right_root[0])
    parts = 4
    left_new, right_new, update = pl.pallas_call(
        functools.partial(write_kernel, parts),
        out_shape=(
            jax.ShapeDtypeStruct(square, bf16),
            jax.ShapeDtypeStruct(square, bf16),
            jax.ShapeDtypeStruct(strips, bf16),
        ),
        in_specs=[vmem_spec] * 3,
        out_specs=(any_spec,) * 3,
        scratch_shapes=[pltpu.SemaphoreType.DMA((3, parts))],
        compiler_params=pltpu.CompilerParams(vmem_limit_bytes=1 << 20),
        name="write_results",
    )(*(pltpu.with_memory_space_constraint(x, pltpu.VMEM) for x in held))
    return left_new[None], right_new[None], update.reshape(gradient.shape)


def solution(mesh):
    return jax.shard_map(
        shards,
        mesh=mesh,
        in_specs=(
            P(None, "tensor", "dp", None),
            P(),
            P(("dp", "tensor"), None, None),
            P(("dp", "tensor"), None, None),
        ),
        out_specs=(
            P(("dp", "tensor"), None, None),
            P(("dp", "tensor"), None, None),
            P(None, "tensor", "dp", None),
        ),
        check_vma=False,
    )
```
